32 devices in a mesh: member: 2 (over x), lon: 16 (over z, y, core).
Axes of the slice: x: 2, y: 2, z: 4, core: 2. Of those that a mesh axis runs over, the one named last changes fastest.
Arguments:
- tracer_field: float32 [16, 2, 192, 768], P('member', None, 'lon'), parts along dimension 0, may hold values from -6 to 6
- courant_lon: float32 [4, 192, 768], P('member', 'lon'), parts along dimension 0, may hold values from -0.4 to 0.4
- courant_lat: float32 [4, 192, 768], P('member', 'lon'), parts along dimension 0, may hold values from -0.4 to 0.4
- diffusivity: float32 [2, 192, 768], P('member', 'lon'), parts along dimension 0, may hold values from 0.1 to 4
- polar_mask: int32 [768], replicated, may hold values from 0 to 1, as said below
- cutoff: int32 [768], replicated, may hold values from 4 to 95, as said below
Outputs:
- updated_field: float32 [16, 2, 192, 768], P('member', None, 'lon'), parts along dimension 0
The draws below stay inside these ranges and needn't reach their ends.
There are 2 independent parts, one for each index of `member`. The reference program is written for one: setup_inputs(seed, part) draws one part's arguments, and reference() takes and returns one part's arrays. A program takes and returns all parts, laid end to end along the dimension named above; an argument that names none is the same for every part. Nothing has to cross between parts.
Inputs may be any that keep to these rules, and one draw needn't show every extreme that they name: `polar_mask`: 1 on the first 128 rows and on a last run of 64 to 128 rows, 0 elsewhere. `cutoff`: only rows with mask 1 use it.
All inputs are finite; a program needn't handle non-finite values.
Results may differ from the reference program's by a relative error of at most 0.00005.
Values sent between devices are 32-bit elements; how exact they have to be, the bound alone decides.
A program may use at most 128 MiB of HBM per device.

```python
import math
import jax
import jax.numpy as jnp

TRACERS = 8
LEVELS = 2
NLAT = 768
NLON = 192
POLAR = 128


def draw_polar_mask(key, part):
    south_rows = jax.random.randint(jax.random.fold_in(key, 11), (), POLAR // 2, POLAR + 1)
    rows_index = jnp.arange(NLAT, dtype=jnp.int32)
    inside = (rows_index < POLAR) | (rows_index >= NLAT - south_rows)
    return jnp.where(inside, 1, 0).astype(jnp.int32)


def draw_cutoff(key, part):
    values = jax.random.randint(jax.random.fold_in(key, 7), (NLAT,), 4, NLON // 2)
    values = values.at[0].set(4).at[NLAT - 1].set(NLON // 2 - 1)
    return values.astype(jnp.int32)


def steps_of(stream_key, shape, cuts, smallest, top_value):
    level = 1.0
    for dim, blocks in cuts:
        draws = jax.random.uniform(jax.random.fold_in(jax.random.fold_in(stream_key, 6), dim), (blocks,), jnp.float32, smallest / len(cuts), top_value / len(cuts))
        level = level * jnp.repeat(jnp.exp(draws), shape[dim] // blocks).reshape((-1,) + (1,) * (len(shape) - 1 - dim))
    return level


def normal_values(own_key, extent, deviation, bound, shards=(), kind=jnp.bfloat16):
    values = jax.random.normal(own_key, extent, jnp.float32) * deviation
    if len(shards) > 0:
        values = steps_of(own_key, extent, shards, -0.22, 0.18) * values
    return jnp.clip(values, min=-bound, max=bound).astype(kind)


def setup_inputs(seed: int = 0, part: int = 0) -> dict:
    key_of = jax.random.split(jax.random.key(seed), 7)
    own_keys = jax.random.split(jax.random.fold_in(key_of[6], part), 7)
    return {
        "tracer_field": normal_values(own_keys[0], (TRACERS, LEVELS, NLON, NLAT), 1.0, 6.0, ((2, 16),), jnp.float32),
        "courant_lon": jnp.clip(jax.random.uniform(own_keys[1], (LEVELS, NLON, NLAT), jnp.float32, -0.4, 0.4) * steps_of(own_keys[1], (LEVELS, NLON, NLAT), ((1, 16),), -0.4, 0.0), -0.4, 0.4),
        "courant_lat": jnp.clip(jax.random.uniform(own_keys[2], (LEVELS, NLON, NLAT), jnp.float32, -0.4, 0.4) * steps_of(own_keys[2], (LEVELS, NLON, NLAT), ((1, 16),), -0.4, 0.0), -0.4, 0.4),
        "diffusivity": jnp.clip(jnp.exp(math.log(4.0) - 3.6888794 * jax.random.uniform(own_keys[3], (LEVELS - 1, NLON, NLAT), jnp.float32) ** steps_of(own_keys[3], (LEVELS - 1, NLON, NLAT), ((1, 16),), -0.2, 0.2)), 0.1, 4.0),
        "polar_mask": draw_polar_mask(jax.random.fold_in(key_of[6], 71), part),
        "cutoff": draw_cutoff(jax.random.fold_in(key_of[6], 71), part),
    }


def advect(tracer, courant_lon, courant_lat):
    right_next = jnp.roll(tracer, -1, axis=2)
    east = jnp.maximum(courant_lon, 0.0)[None] * tracer + jnp.minimum(courant_lon, 0.0)[None] * right_next
    west = jnp.roll(east, 1, axis=2)
    zero_row = jnp.zeros_like(tracer[..., :1])
    north_next = jnp.concatenate([tracer[..., 1:], zero_row], axis=3)
    north = jnp.maximum(courant_lat, 0.0)[None] * tracer + jnp.minimum(courant_lat, 0.0)[None] * north_next
    south = jnp.concatenate([zero_row, north[..., :-1]], axis=3)
    return tracer - (east - west) - (north - south)


def vertical_solve(diffusivity, field):
    levels = field.shape[1]
    zeros_plane = jnp.zeros_like(diffusivity[0])
    upper_list = []
    rhs_list = []
    prev_upper = None
    prev_rhs = None
    for lev_index in range(levels):
        below = diffusivity[lev_index - 1] if lev_index > 0 else zeros_plane
        above = diffusivity[lev_index] if lev_index < levels - 1 else zeros_plane
        diagonal = 1.0 + below + above
        source = field[:, lev_index]
        if lev_index == 0:
            denom = diagonal
            new_rhs = source / denom
        else:
            denom = diagonal + below * prev_upper
            new_rhs = (source + below * prev_rhs) / denom
        new_upper = -above / denom
        upper_list.append(new_upper)
        rhs_list.append(new_rhs)
        prev_upper = new_upper
        prev_rhs = new_rhs
    result = [None] * levels
    current = rhs_list[levels - 1]
    result[levels - 1] = current
    for lev_index in range(levels - 2, -1, -1):
        current = rhs_list[lev_index] - upper_list[lev_index] * current
        result[lev_index] = current
    return jnp.stack(result, axis=1)


def reference(tracer_field, courant_lon, courant_lat, diffusivity, polar_mask, cutoff):
    advected = advect(tracer_field, courant_lon, courant_lat)
    spectrum = jnp.fft.rfft(advected, axis=2)
    modes = jnp.arange(NLON // 2 + 1, dtype=jnp.int32)
    keep_high = (modes[:, None] > cutoff[None, :])
    high = jnp.fft.irfft(spectrum * keep_high, n=NLON, axis=2).astype(advected.dtype)
    filtered = advected - high * polar_mask.astype(advected.dtype)[None, None, None, :]
    return vertical_solve(diffusivity, filtered)
```

```python
import functools
import math

import jax
import jax.numpy as jnp
import numpy as np
from jax import lax
from jax.experimental import pallas as pl
from jax.experimental.layout import Layout, with_layout_constraint
from jax.experimental.pallas import tpu as pltpu
from jax.sharding import PartitionSpec as P

POLAR = 128
LANES = 128


def padded(x, sides, width):
    for axis, dim in sides:
        size, length = (lax.axis_size(axis), x.shape[dim])
        up = [(i, (i + 1) % size) for i in range(size)]
        down = [(j, i) for i, j in up]
        last = lax.slice_in_dim(x, length - width, length, axis=dim)
        leading = lax.slice_in_dim(x, 0, width, axis=dim)
        before = lax.ppermute(last, axis, up)
        after = lax.ppermute(leading, axis, down)
        x = jnp.concatenate([before, x, after], axis=dim)
    return x


def fourier_tables(length):
    half_len = length // 2
    column = jnp.arange(length, dtype=jnp.int32)[:, None]
    wavenum = jnp.arange(1, half_len + 1, dtype=jnp.int32)[None, :]
    phase = column * wavenum % length
    angle = 2.0 * math.pi / length * phase.astype(jnp.float32)
    return (jnp.cos(angle), jnp.sin(angle))


def high_part(block, row_cut, cosine, sine):
    length = block.shape[1]
    half_len = length // 2
    highest = lax.Precision.HIGHEST
    real_part = jnp.einsum("bir,im->brm", block, cosine, precision=highest)
    imag_part = jnp.einsum("bir,im->brm", block, sine, precision=highest)
    wavenum = jnp.arange(1, half_len + 1, dtype=jnp.int32)
    weights = jnp.where(wavenum == half_len, 1.0 / length, 2.0 / length).astype(jnp.float32)
    keeper = jnp.where(wavenum[None, :] > row_cut[:, None], weights[None, :], 0.0)
    return jnp.einsum(
        "brm,im->bir", real_part * keeper[None], cosine, precision=highest
    ) + jnp.einsum("brm,im->bir", imag_part * keeper[None], sine, precision=highest)


def local_by_collectives(tracer_field, courant_lon, courant_lat, diffusivity, polar_mask, cutoff):
    tracers, levels, lon_local, lat_rows = tracer_field.shape
    zero_row = jnp.zeros_like(tracer_field[..., :1])
    north_next = jnp.concatenate([tracer_field[..., 1:], zero_row], axis=3)
    north = (
        jnp.maximum(courant_lat, 0.0)[None] * tracer_field
        + jnp.minimum(courant_lat, 0.0)[None] * north_next
    )
    south = jnp.concatenate([zero_row, north[..., :-1]], axis=3)
    stacked = jnp.concatenate([tracer_field, courant_lon[None]], axis=0)
    extended = padded(stacked, (("lon", 2),), 1)
    tracer_ext = extended[:tracers]
    speed_ext = extended[tracers][None, :, :-1]
    east_all = (
        jnp.maximum(speed_ext, 0.0) * tracer_ext[:, :, :-1]
        + jnp.minimum(speed_ext, 0.0) * tracer_ext[:, :, 1:]
    )
    advected = tracer_field - (east_all[:, :, 1:] - east_all[:, :, :-1]) - (north - south)
    batched = advected.reshape(tracers * levels, lon_local, lat_rows)
    ends = jnp.concatenate([batched[..., :POLAR], batched[..., lat_rows - POLAR :]], axis=2)
    ends_mask = jnp.concatenate([polar_mask[:POLAR], polar_mask[lat_rows - POLAR :]])
    ends_cut = jnp.concatenate([cutoff[:POLAR], cutoff[lat_rows - POLAR :]])
    size = lax.axis_size("lon")
    cosine, sine = fourier_tables(lon_local * size)
    row_count = 2 * POLAR // size
    first_row = lax.axis_index("lon") * row_count
    my_cut = lax.dynamic_slice_in_dim(ends_cut, first_row, row_count)
    my_mask = lax.dynamic_slice_in_dim(ends_mask.astype(jnp.float32), first_row, row_count)
    removed = (
        high_part(
            lax.all_to_all(ends, "lon", split_axis=2, concat_axis=1, tiled=True),
            my_cut,
            cosine,
            sine,
        )
        * my_mask[None, None, :]
    )
    correction = lax.all_to_all(removed, "lon", split_axis=1, concat_axis=2, tiled=True)
    filtered = jnp.concatenate(
        [
            batched[..., :POLAR] - correction[..., :POLAR],
            batched[..., POLAR : lat_rows - POLAR],
            batched[..., lat_rows - POLAR :] - correction[..., POLAR:],
        ],
        axis=2,
    ).reshape(tracers, levels, lon_local, lat_rows)
    share = diffusivity[0] / (1.0 + 2.0 * diffusivity[0])
    moved = share[None] * (filtered[:, 1] - filtered[:, 0])
    return jnp.stack([filtered[:, 0] + moved, filtered[:, 1] - moved], axis=1)


def orthonormal_rows(length):
    half = length // 2
    wave = np.arange(1, half + 1)[:, None]
    angle = 2.0 * np.pi / length * (wave * np.arange(length)[None, :] % length)
    scale = np.sqrt(np.where(wave == half, 1.0, 2.0) / length)
    return np.concatenate([np.cos(angle) * scale, np.sin(angle) * scale], axis=0)


def split(x):
    high = x.astype(jnp.bfloat16)
    return high, (x - high.astype(jnp.float32)).astype(jnp.bfloat16)


def product(a_high, a_low, b):
    b_high, b_low = split(b)
    dot = functools.partial(jnp.dot, preferred_element_type=jnp.float32)
    return dot(a_high, b_high) + (dot(a_high, b_low) + dot(a_low, b_high))


def kernel(
    n, tracers, lons, blocks,
    t_hbm, c_hbm, cl_hbm, kd_hbm, cut_hbm, mask_hbm, g_hbm, o_hbm,
    buf, clv, kv, cutv, maskv, gv, coef, adv, out_blocks, in_blocks, spec, back_blocks, corr,
    in_sem, halo_send, halo_recv, send_sem, recv_sem, back_send, back_recv, out_sem,
):
    rows = lons * blocks * 2
    stride = blocks * 2
    top = 16
    me = lax.axis_index("lon")
    right, left = lax.rem(me + 1, n), lax.rem(me + n - 1, n)
    my_pair = me // 2
    half = lax.rem(me, 2)

    loads = [
        pltpu.make_async_copy(c_hbm, buf.at[tracers, pl.ds(top, rows)], in_sem.at[0]),
        pltpu.make_async_copy(cl_hbm, clv.at[pl.ds(8, rows)], in_sem.at[1]),
        pltpu.make_async_copy(t_hbm, buf.at[pl.ds(0, tracers), pl.ds(top, rows)], in_sem.at[2]),
        pltpu.make_async_copy(kd_hbm, kv, in_sem.at[3]),
        pltpu.make_async_copy(cut_hbm, cutv, in_sem.at[4]),
        pltpu.make_async_copy(mask_hbm, maskv, in_sem.at[5]),
        pltpu.make_async_copy(g_hbm, gv, in_sem.at[6]),
    ]
    for load in loads:
        load.start()

    barrier = pltpu.get_barrier_semaphore()

    @pl.loop(1, n)
    def _(k):
        pl.semaphore_signal(barrier, inc=1, device_id={"lon": lax.rem(me + k, n)}, device_id_type=pl.DeviceIdType.MESH)

    pl.semaphore_wait(barrier, n - 1)

    def remote(src, dst, send, recv, to):
        return pltpu.make_async_remote_copy(
            src_ref=src, dst_ref=dst, send_sem=send, recv_sem=recv,
            device_id={"lon": to}, device_id_type=pl.DeviceIdType.MESH,
        )

    halos = [
        remote(c_hbm.at[pl.ds(rows - 16, 16)], buf.at[tracers, pl.ds(0, 16)], halo_send.at[0], halo_recv.at[0], right),
        remote(t_hbm.at[:, pl.ds(rows - 16, 16)], buf.at[pl.ds(0, tracers), pl.ds(0, 16)], halo_send.at[1], halo_recv.at[1], right),
        remote(t_hbm.at[:, pl.ds(0, 16)], buf.at[pl.ds(0, tracers), pl.ds(top + rows, 16)], halo_send.at[2], halo_recv.at[2], left),
    ]
    for halo in halos:
        halo.start()

    clv[pl.ds(0, 8)] = jnp.zeros((8, LANES), jnp.float32)
    loads[1].wait()
    row = lax.rem(lax.broadcasted_iota(jnp.int32, (rows, LANES), 0), stride)
    lane = lax.broadcasted_iota(jnp.int32, (rows, LANES), 1)
    last_lane, first_lane = lane == LANES - 1, lane == 0
    cl = clv[pl.ds(8, rows)]
    cl_prev = pltpu.roll(jnp.where(last_lane, clv[pl.ds(6, rows)], cl), 1, axis=1)
    cl_prev = jnp.where((row < 2) & first_lane, 0.0, cl_prev)
    north_next = jnp.where((row >= stride - 2) & last_lane, 0.0, jnp.minimum(cl, 0.0))
    coef[3] = -north_next
    coef[4] = jnp.maximum(cl_prev, 0.0)
    rest = 1.0 - jnp.maximum(cl, 0.0) + jnp.minimum(cl_prev, 0.0)
    loads[0].wait()
    halos[0].wait_recv()
    c = buf[tracers, pl.ds(top, rows)]
    c_west = buf[tracers, pl.ds(top - stride, rows)]
    coef[0] = rest - jnp.maximum(c, 0.0) + jnp.minimum(c_west, 0.0)
    coef[1] = -jnp.minimum(c, 0.0)
    coef[2] = jnp.maximum(c_west, 0.0)
    loads[2].wait()
    halos[1].wait_recv()
    halos[2].wait_recv()

    def send(dest):
        return remote(out_blocks.at[dest], in_blocks.at[me], send_sem.at[dest], recv_sem.at[me], dest)

    def advect(t):
        x = buf[t, pl.ds(top, rows)]
        y = jnp.where(first_lane, buf[t, pl.ds(top + 2, rows)], x)
        total = coef[0] * x + coef[3] * pltpu.roll(y, LANES - 1, axis=1)
        y = jnp.where(last_lane, buf[t, pl.ds(top - 2, rows)], x)
        total += coef[4] * pltpu.roll(y, 1, axis=1)
        total += coef[1] * buf[t, pl.ds(top + stride, rows)]
        total += coef[2] * buf[t, pl.ds(top - stride, rows)]
        adv[t] = total
        for h in range(2):
            for lev in range(2):
                first = h * (stride - 2) + lev
                out_blocks[2 * t + h, pl.ds(lev * lons, lons)] = adv[t, pl.ds(first, lons, stride=stride)]

    @pl.loop(1, tracers)
    def _(i):
        t = lax.rem(my_pair + i, tracers)
        advect(t)
        send(2 * t).start()
        send(2 * t + 1).start()

    advect(my_pair)
    twin = 2 * my_pair + 1 - half
    send(twin).start()
    in_blocks[me] = out_blocks[me]

    loads[3].wait()
    k = kv[...]
    kv[...] = k / (1.0 + 2.0 * k)

    def solve(t, block, remove):
        share = kv[pl.ds(block, lons, stride=blocks)]
        at = [pl.ds(2 * block + lev, lons, stride=stride) for lev in range(2)]
        upper, lower = adv[t, at[0]], adv[t, at[1]]
        if remove is not None:
            upper = upper - corr[remove, pl.ds(0, lons)]
            lower = lower - corr[remove, pl.ds(lons, lons)]
        moved = share * (lower - upper)
        adv[t, at[0]] = upper + moved
        adv[t, at[1]] = lower - moved

    @pl.loop(0, tracers)
    def _(t):
        for block in range(1, blocks - 1):
            solve(t, block, None)

    for load in loads[4:]:
        load.wait()

    def received(s):
        return remote(out_blocks.at[s], in_blocks.at[s], send_sem.at[s], recv_sem.at[s], s)

    @pl.loop(1, n)
    def _(k):
        received(lax.rem(me + n - k, n)).wait_recv()

    for s in range(n):
        for lev in range(2):
            spec[pl.ds(s * lons, lons), pl.ds(lev * LANES, LANES)] = in_blocks[s, pl.ds(lev * lons, lons)]

    length = n * lons
    cut = jnp.where(half == 0, cutv[pl.ds(0, LANES)], cutv[pl.ds((blocks - 1) * LANES, LANES)])
    mask = jnp.where(half == 0, maskv[pl.ds(0, LANES)], maskv[pl.ds((blocks - 1) * LANES, LANES)])
    cut = jnp.where(mask == 1, cut, length).reshape(1, LANES)
    wave = lax.rem(lax.broadcasted_iota(jnp.int32, (length, LANES), 0), length // 2) + 1
    keep = wave > cut
    waves = product(gv[0], gv[1], spec[...])
    waves = jnp.where(jnp.concatenate([keep, keep], axis=1), waves, 0.0)
    spec[...] = product(gv[2], gv[3], waves)
    for s in range(n):
        for lev in range(2):
            back_blocks[s, pl.ds(lev * lons, lons)] = spec[pl.ds(s * lons, lons), pl.ds(lev * LANES, LANES)]

    def back(dest):
        return remote(back_blocks.at[dest], corr.at[me], back_send.at[dest], back_recv.at[me], dest)

    @pl.loop(1, n)
    def _(k):
        back(lax.rem(me + k, n)).start()

    corr[me] = back_blocks[me]

    def returned(s):
        return remote(back_blocks.at[s], corr.at[s], back_send.at[s], back_recv.at[s], s)

    def finish(t):
        solve(t, 0, 2 * t)
        solve(t, blocks - 1, 2 * t + 1)
        pltpu.make_async_copy(adv.at[t], o_hbm.at[t], out_sem.at[t]).start()

    returned(twin).wait_recv()
    finish(my_pair)

    @pl.loop(1, tracers)
    def _(i):
        t = lax.rem(my_pair + tracers - i, tracers)
        returned(2 * t).wait_recv()
        returned(2 * t + 1).wait_recv()
        finish(t)

    for halo in halos:
        halo.wait_send()

    @pl.loop(1, n)
    def _(k):
        dest = lax.rem(me + k, n)
        send(dest).wait_send()
        back(dest).wait_send()

    @pl.loop(0, tracers)
    def _(t):
        pltpu.make_async_copy(adv.at[t], o_hbm.at[t], out_sem.at[t]).wait()


def flat_rows(x):
    count, levels, lons, lat_rows = x.shape
    x = x.transpose(0, 2, 1, 3).reshape(count, lons, levels, lat_rows // LANES, LANES)
    x = with_layout_constraint(x, Layout((0, 1, 3, 2, 4)))
    return x.transpose(0, 1, 3, 2, 4).reshape(count, lons * lat_rows // LANES * levels, LANES)


def local_by_kernel(n, tracer_field, courant_lon, courant_lat, diffusivity, polar_mask, cutoff):
    tracers, levels, lons, lat_rows = tracer_field.shape
    blocks = lat_rows // LANES
    rows = lons * blocks * levels
    field = flat_rows(tracer_field)
    speeds = [flat_rows(x[None])[0] for x in (courant_lon, courant_lat)]
    length = n * lons
    g = orthonormal_rows(length).astype(np.float32)
    tables = []
    for x in (g, g.T):
        high = x.astype(jnp.bfloat16)
        tables += [high, (x - high.astype(np.float32)).astype(jnp.bfloat16)]
    f32 = jnp.float32
    result = pl.pallas_call(
        functools.partial(kernel, n, tracers, lons, blocks),
        out_shape=jax.ShapeDtypeStruct((tracers, rows, LANES), f32),
        in_specs=[pl.BlockSpec(memory_space=pl.ANY)] * 7,
        out_specs=pl.BlockSpec(memory_space=pl.ANY),
        scratch_shapes=[
            pltpu.VMEM((tracers + 1, rows + 32, LANES), f32),
            pltpu.VMEM((rows + 8, LANES), f32),
            pltpu.VMEM((lons * blocks, LANES), f32),
            pltpu.VMEM((lat_rows,), jnp.int32),
            pltpu.VMEM((lat_rows,), jnp.int32),
            pltpu.VMEM((4, length, length), jnp.bfloat16),
            pltpu.VMEM((5, rows, LANES), f32),
            pltpu.VMEM((tracers, rows, LANES), f32),
            pltpu.VMEM((n, 2 * lons, LANES), f32),
            pltpu.VMEM((n, 2 * lons, LANES), f32),
            pltpu.VMEM((length, 2 * LANES), f32),
            pltpu.VMEM((n, 2 * lons, LANES), f32),
            pltpu.VMEM((n, 2 * lons, LANES), f32),
            pltpu.SemaphoreType.DMA((7,)),
            pltpu.SemaphoreType.DMA((3,)),
            pltpu.SemaphoreType.DMA((3,)),
            pltpu.SemaphoreType.DMA((n,)),
            pltpu.SemaphoreType.DMA((n,)),
            pltpu.SemaphoreType.DMA((n,)),
            pltpu.SemaphoreType.DMA((n,)),
            pltpu.SemaphoreType.DMA((tracers,)),
        ],
        compiler_params=pltpu.CompilerParams(collective_id=0, has_side_effects=True),
    )(
        field,
        *speeds,
        diffusivity.reshape(lons * blocks, LANES),
        cutoff,
        polar_mask,
        jnp.asarray(np.stack(tables)),
    )
    result = result.reshape(tracers, lons, blocks, levels, LANES).transpose(0, 1, 3, 2, 4)
    return result.reshape(tracers, lons, levels, lat_rows).transpose(0, 2, 1, 3)


def solution(mesh):
    n = mesh.shape["lon"]
    members = mesh.shape["member"]
    placed = (
        P("member", None, "lon", None),
        P("member", "lon", None),
        P("member", "lon", None),
        P("member", "lon", None),
        P(),
        P(),
    )

    def run(tracer_field, *rest):
        tracers, levels, length, lat_rows = tracer_field.shape
        fits = (
            n == 2 * (tracers // members)
            and levels == 2
            and lat_rows % LANES == 0
            and (length // n) * (lat_rows // LANES) % 4 == 0
            and lat_rows // LANES <= 8
        )
        local = functools.partial(local_by_kernel, n) if fits else local_by_collectives
        return jax.shard_map(
            local, mesh=mesh, in_specs=placed, out_specs=P("member", None, "lon", None), check_vma=False
        )(tracer_field, *rest)

    return run
```

```python
import functools
import math

import jax
import jax.numpy as jnp
import numpy as np
from jax import lax
from jax.experimental import pallas as pl
from jax.experimental.layout import Layout, with_layout_constraint
from jax.experimental.pallas import tpu as pltpu
from jax.sharding import PartitionSpec as P

POLAR = 128
LANES = 128


def padded(x, sides, width):
    for axis, dim in sides:
        size, length = (lax.axis_size(axis), x.shape[dim])
        up = [(i, (i + 1) % size) for i in range(size)]
        down = [(j, i) for i, j in up]
        last = lax.slice_in_dim(x, length - width, length, axis=dim)
        leading = lax.slice_in_dim(x, 0, width, axis=dim)
        before = lax.ppermute(last, axis, up)
        after = lax.ppermute(leading, axis, down)
        x = jnp.concatenate([before, x, after], axis=dim)
    return x


def fourier_tables(length):
    half_len = length // 2
    column = jnp.arange(length, dtype=jnp.int32)[:, None]
    wavenum = jnp.arange(1, half_len + 1, dtype=jnp.int32)[None, :]
    phase = column * wavenum % length
    angle = 2.0 * math.pi / length * phase.astype(jnp.float32)
    return (jnp.cos(angle), jnp.sin(angle))


def high_part(block, row_cut, cosine, sine):
    length = block.shape[1]
    half_len = length // 2
    highest = lax.Precision.HIGHEST
    real_part = jnp.einsum("bir,im->brm", block, cosine, precision=highest)
    imag_part = jnp.einsum("bir,im->brm", block, sine, precision=highest)
    wavenum = jnp.arange(1, half_len + 1, dtype=jnp.int32)
    weights = jnp.where(wavenum == half_len, 1.0 / length, 2.0 / length).astype(jnp.float32)
    keeper = jnp.where(wavenum[None, :] > row_cut[:, None], weights[None, :], 0.0)
    return jnp.einsum(
        "brm,im->bir", real_part * keeper[None], cosine, precision=highest
    ) + jnp.einsum("brm,im->bir", imag_part * keeper[None], sine, precision=highest)


def local_by_collectives(tracer_field, courant_lon, courant_lat, diffusivity, polar_mask, cutoff):
    tracers, levels, lon_local, lat_rows = tracer_field.shape
    zero_row = jnp.zeros_like(tracer_field[..., :1])
    north_next = jnp.concatenate([tracer_field[..., 1:], zero_row], axis=3)
    north = (
        jnp.maximum(courant_lat, 0.0)[None] * tracer_field
        + jnp.minimum(courant_lat, 0.0)[None] * north_next
    )
    south = jnp.concatenate([zero_row, north[..., :-1]], axis=3)
    stacked = jnp.concatenate([tracer_field, courant_lon[None]], axis=0)
    extended = padded(stacked, (("lon", 2),), 1)
    tracer_ext = extended[:tracers]
    speed_ext = extended[tracers][None, :, :-1]
    east_all = (
        jnp.maximum(speed_ext, 0.0) * tracer_ext[:, :, :-1]
        + jnp.minimum(speed_ext, 0.0) * tracer_ext[:, :, 1:]
    )
    advected = tracer_field - (east_all[:, :, 1:] - east_all[:, :, :-1]) - (north - south)
    batched = advected.reshape(tracers * levels, lon_local, lat_rows)
    ends = jnp.concatenate([batched[..., :POLAR], batched[..., lat_rows - POLAR :]], axis=2)
    ends_mask = jnp.concatenate([polar_mask[:POLAR], polar_mask[lat_rows - POLAR :]])
    ends_cut = jnp.concatenate([cutoff[:POLAR], cutoff[lat_rows - POLAR :]])
    size = lax.axis_size("lon")
    cosine, sine = fourier_tables(lon_local * size)
    row_count = 2 * POLAR // size
    first_row = lax.axis_index("lon") * row_count
    my_cut = lax.dynamic_slice_in_dim(ends_cut, first_row, row_count)
    my_mask = lax.dynamic_slice_in_dim(ends_mask.astype(jnp.float32), first_row, row_count)
    removed = (
        high_part(
            lax.all_to_all(ends, "lon", split_axis=2, concat_axis=1, tiled=True),
            my_cut,
            cosine,
            sine,
        )
        * my_mask[None, None, :]
    )
    correction = lax.all_to_all(removed, "lon", split_axis=1, concat_axis=2, tiled=True)
    filtered = jnp.concatenate(
        [
            batched[..., :POLAR] - correction[..., :POLAR],
            batched[..., POLAR : lat_rows - POLAR],
            batched[..., lat_rows - POLAR :] - correction[..., POLAR:],
        ],
        axis=2,
    ).reshape(tracers, levels, lon_local, lat_rows)
    share = diffusivity[0] / (1.0 + 2.0 * diffusivity[0])
    moved = share[None] * (filtered[:, 1] - filtered[:, 0])
    return jnp.stack([filtered[:, 0] + moved, filtered[:, 1] - moved], axis=1)


def orthonormal_rows(length):
    half = length // 2
    wave = np.arange(1, half + 1)[:, None]
    angle = 2.0 * np.pi / length * (wave * np.arange(length)[None, :] % length)
    scale = np.sqrt(np.where(wave == half, 1.0, 2.0) / length)
    return np.concatenate([np.cos(angle) * scale, np.sin(angle) * scale], axis=0)


def split(x):
    high = x.astype(jnp.bfloat16)
    return high, (x - high.astype(jnp.float32)).astype(jnp.bfloat16)


def product(a_high, a_low, b):
    b_high, b_low = split(b)
    dot = functools.partial(jnp.dot, preferred_element_type=jnp.float32)
    return dot(a_high, b_high) + (dot(a_high, b_low) + dot(a_low, b_high))


def kernel(
    n, tracers, lons, blocks,
    t_hbm, c_hbm, cl_hbm, kd_hbm, cut_hbm, mask_hbm, g_hbm, gt_hbm, o_hbm,
    buf, clv, kv, cutv, maskv, gv, gtv, coef, adv, out_blocks, in_blocks, spec, back_blocks, corr,
    in_sem, halo_send, halo_recv, send_sem, recv_sem, back_send, back_recv, out_sem,
):
    rows = lons * blocks * 2
    stride = blocks * 2
    top = 16
    slot = spec.shape[0] // n
    me = lax.axis_index("lon")
    right, left = lax.rem(me + 1, n), lax.rem(me + n - 1, n)
    my_pair = me // 2
    half = lax.rem(me, 2)

    loads = [
        pltpu.make_async_copy(c_hbm, buf.at[tracers, pl.ds(top, rows)], in_sem.at[0]),
        pltpu.make_async_copy(cl_hbm, clv.at[pl.ds(8, rows)], in_sem.at[1]),
        pltpu.make_async_copy(t_hbm, buf.at[pl.ds(0, tracers), pl.ds(top, rows)], in_sem.at[2]),
        pltpu.make_async_copy(kd_hbm, kv, in_sem.at[3]),
        pltpu.make_async_copy(cut_hbm, cutv, in_sem.at[4]),
        pltpu.make_async_copy(mask_hbm, maskv, in_sem.at[5]),
        pltpu.make_async_copy(g_hbm, gv, in_sem.at[6]),
        pltpu.make_async_copy(gt_hbm, gtv, in_sem.at[7]),
    ]
    for load in loads:
        load.start()

    barrier = pltpu.get_barrier_semaphore()

    @pl.loop(1, n)
    def _(k):
        pl.semaphore_signal(barrier, inc=1, device_id={"lon": lax.rem(me + k, n)}, device_id_type=pl.DeviceIdType.MESH)

    pl.semaphore_wait(barrier, n - 1)

    def remote(src, dst, send, recv, to):
        return pltpu.make_async_remote_copy(
            src_ref=src, dst_ref=dst, send_sem=send, recv_sem=recv,
            device_id={"lon": to}, device_id_type=pl.DeviceIdType.MESH,
        )

    halos = [
        remote(c_hbm.at[pl.ds(rows - 16, 16)], buf.at[tracers, pl.ds(0, 16)], halo_send.at[0], halo_recv.at[0], right),
        remote(t_hbm.at[:, pl.ds(rows - 16, 16)], buf.at[pl.ds(0, tracers), pl.ds(0, 16)], halo_send.at[1], halo_recv.at[1], right),
        remote(t_hbm.at[:, pl.ds(0, 16)], buf.at[pl.ds(0, tracers), pl.ds(top + rows, 16)], halo_send.at[2], halo_recv.at[2], left),
    ]
    for halo in halos:
        halo.start()

    spec[...] = jnp.zeros_like(spec)
    clv[pl.ds(0, 8)] = jnp.zeros((8, LANES), jnp.float32)
    loads[1].wait()
    row = lax.rem(lax.broadcasted_iota(jnp.int32, (rows, LANES), 0), stride)
    lane = lax.broadcasted_iota(jnp.int32, (rows, LANES), 1)
    last_lane, first_lane = lane == LANES - 1, lane == 0
    cl = clv[pl.ds(8, rows)]
    cl_prev = pltpu.roll(jnp.where(last_lane, clv[pl.ds(6, rows)], cl), 1, axis=1)
    cl_prev = jnp.where((row < 2) & first_lane, 0.0, cl_prev)
    north_next = jnp.where((row >= stride - 2) & last_lane, 0.0, jnp.minimum(cl, 0.0))
    coef[3] = -north_next
    coef[4] = jnp.maximum(cl_prev, 0.0)
    rest = 1.0 - jnp.maximum(cl, 0.0) + jnp.minimum(cl_prev, 0.0)
    loads[0].wait()
    halos[0].wait_recv()
    c = buf[tracers, pl.ds(top, rows)]
    c_west = buf[tracers, pl.ds(top - stride, rows)]
    coef[0] = rest - jnp.maximum(c, 0.0) + jnp.minimum(c_west, 0.0)
    coef[1] = -jnp.minimum(c, 0.0)
    coef[2] = jnp.maximum(c_west, 0.0)
    loads[2].wait()
    halos[1].wait_recv()
    halos[2].wait_recv()

    def send(dest):
        return remote(out_blocks.at[dest], in_blocks.at[me], send_sem.at[dest], recv_sem.at[me], dest)

    def advect(t):
        x = buf[t, pl.ds(top, rows)]
        y = jnp.where(first_lane, buf[t, pl.ds(top + 2, rows)], x)
        total = coef[0] * x + coef[3] * pltpu.roll(y, LANES - 1, axis=1)
        y = jnp.where(last_lane, buf[t, pl.ds(top - 2, rows)], x)
        total += coef[4] * pltpu.roll(y, 1, axis=1)
        total += coef[1] * buf[t, pl.ds(top + stride, rows)]
        total += coef[2] * buf[t, pl.ds(top - stride, rows)]
        adv[t] = total
        for h in range(2):
            for lev in range(2):
                first = h * (stride - 2) + lev
                out_blocks[2 * t + h, pl.ds(lev * lons, lons)] = adv[t, pl.ds(first, lons, stride=stride)]

    def pair_at(i):
        offset = tracers // 2 + (1 - 2 * lax.rem(i, 2)) * ((i + 1) // 2)
        return lax.rem(my_pair + offset, tracers)

    @pl.loop(0, tracers - 1)
    def _(i):
        t = pair_at(i)
        advect(t)
        send(2 * t).start()
        send(2 * t + 1).start()

    advect(my_pair)
    twin = 2 * my_pair + 1 - half
    send(twin).start()
    in_blocks[me] = out_blocks[me]

    loads[3].wait()
    k = kv[...]
    kv[...] = k / (1.0 + 2.0 * k)

    def solve(t, block, remove):
        share = kv[pl.ds(block, lons, stride=blocks)]
        at = [pl.ds(2 * block + lev, lons, stride=stride) for lev in range(2)]
        upper, lower = adv[t, at[0]], adv[t, at[1]]
        if remove is not None:
            upper = upper - corr[remove, pl.ds(0, lons)]
            lower = lower - corr[remove, pl.ds(lons, lons)]
        moved = share * (lower - upper)
        adv[t, at[0]] = upper + moved
        adv[t, at[1]] = lower - moved

    @pl.loop(0, tracers)
    def _(t):
        for block in range(1, blocks - 1):
            solve(t, block, None)

    for load in loads[4:]:
        load.wait()

    def received(s):
        return remote(out_blocks.at[s], in_blocks.at[s], send_sem.at[s], recv_sem.at[s], s)

    def pack(s):
        first = pl.multiple_of(s * slot, slot)
        for lev in range(2):
            spec[pl.ds(first, lons), pl.ds(lev * LANES, LANES)] = in_blocks[s, pl.ds(lev * lons, lons)]

    length = n * lons
    cut = jnp.where(half == 0, cutv[pl.ds(0, LANES)], cutv[pl.ds((blocks - 1) * LANES, LANES)])
    mask = jnp.where(half == 0, maskv[pl.ds(0, LANES)], maskv[pl.ds((blocks - 1) * LANES, LANES)])
    cut = jnp.where(mask == 1, cut, length).reshape(1, LANES)
    wave = lax.rem(lax.broadcasted_iota(jnp.int32, (length, LANES), 0), length // 2) + 1
    keep = wave > cut
    pack(me)
    received(twin).wait_recv()
    pack(twin)

    @pl.loop(0, tracers - 1)
    def _(i):
        pair = pair_at(tracers - 2 - i)
        for h in range(2):
            received(2 * pair + h).wait_recv()
            pack(2 * pair + h)

    waves = product(gv[0], gv[1], spec[...])
    waves = jnp.where(jnp.concatenate([keep, keep], axis=1), waves, 0.0)
    spec[...] = product(gtv[0], gtv[1], waves)
    def unpack(s):
        first = pl.multiple_of(s * slot, slot)
        for lev in range(2):
            back_blocks[s, pl.ds(lev * lons, lons)] = spec[pl.ds(first, lons), pl.ds(lev * LANES, LANES)]

    def back(dest):
        return remote(back_blocks.at[dest], corr.at[me], back_send.at[dest], back_recv.at[me], dest)

    @pl.loop(0, tracers - 1)
    def _(i):
        pair = pair_at(i)
        for h in range(2):
            unpack(2 * pair + h)
            back(2 * pair + h).start()

    unpack(twin)
    back(twin).start()
    unpack(me)

    corr[me] = back_blocks[me]

    def returned(s):
        return remote(back_blocks.at[s], corr.at[s], back_send.at[s], back_recv.at[s], s)

    def finish(t):
        solve(t, 0, 2 * t)
        solve(t, blocks - 1, 2 * t + 1)
        pltpu.make_async_copy(adv.at[t], o_hbm.at[t], out_sem.at[t]).start()

    returned(twin).wait_recv()
    finish(my_pair)

    @pl.loop(0, tracers - 1)
    def _(i):
        t = pair_at(tracers - 2 - i)
        returned(2 * t).wait_recv()
        returned(2 * t + 1).wait_recv()
        finish(t)

    for halo in halos:
        halo.wait_send()

    @pl.loop(1, n)
    def _(k):
        dest = lax.rem(me + k, n)
        send(dest).wait_send()
        back(dest).wait_send()

    @pl.loop(0, tracers)
    def _(t):
        pltpu.make_async_copy(adv.at[t], o_hbm.at[t], out_sem.at[t]).wait()


def flat_rows(x):
    count, levels, lons, lat_rows = x.shape
    x = x.transpose(0, 2, 1, 3).reshape(count, lons, levels, lat_rows // LANES, LANES)
    x = with_layout_constraint(x, Layout((0, 1, 3, 2, 4)))
    return x.transpose(0, 1, 3, 2, 4).reshape(count, lons * lat_rows // LANES * levels, LANES)


def local_by_kernel(n, tracer_field, courant_lon, courant_lat, diffusivity, polar_mask, cutoff):
    tracers, levels, lons, lat_rows = tracer_field.shape
    blocks = lat_rows // LANES
    rows = lons * blocks * levels
    field = flat_rows(tracer_field)
    speeds = [flat_rows(x[None])[0] for x in (courant_lon, courant_lat)]
    length = n * lons
    g = orthonormal_rows(length).astype(np.float32)
    slot = -(-lons // 8) * 8
    wide = np.zeros((length, n, slot), np.float32)
    wide[:, :, :lons] = g.reshape(length, n, lons)
    wide = wide.reshape(length, n * slot)
    high = wide.astype(jnp.bfloat16)
    table = np.stack([high, (wide - high.astype(np.float32)).astype(jnp.bfloat16)])
    f32 = jnp.float32
    result = pl.pallas_call(
        functools.partial(kernel, n, tracers, lons, blocks),
        out_shape=jax.ShapeDtypeStruct((tracers, rows, LANES), f32),
        in_specs=[pl.BlockSpec(memory_space=pl.ANY)] * 8,
        out_specs=pl.BlockSpec(memory_space=pl.ANY),
        scratch_shapes=[
            pltpu.VMEM((tracers + 1, rows + 32, LANES), f32),
            pltpu.VMEM((rows + 8, LANES), f32),
            pltpu.VMEM((lons * blocks, LANES), f32),
            pltpu.VMEM((lat_rows,), jnp.int32),
            pltpu.VMEM((lat_rows,), jnp.int32),
            pltpu.VMEM((2, length, n * slot), jnp.bfloat16),
            pltpu.VMEM((2, n * slot, length), jnp.bfloat16),
            pltpu.VMEM((5, rows, LANES), f32),
            pltpu.VMEM((tracers, rows, LANES), f32),
            pltpu.VMEM((n, 2 * lons, LANES), f32),
            pltpu.VMEM((n, 2 * lons, LANES), f32),
            pltpu.VMEM((n * slot, 2 * LANES), f32),
            pltpu.VMEM((n, 2 * lons, LANES), f32),
            pltpu.VMEM((n, 2 * lons, LANES), f32),
            pltpu.SemaphoreType.DMA((8,)),
            pltpu.SemaphoreType.DMA((3,)),
            pltpu.SemaphoreType.DMA((3,)),
            pltpu.SemaphoreType.DMA((n,)),
            pltpu.SemaphoreType.DMA((n,)),
            pltpu.SemaphoreType.DMA((n,)),
            pltpu.SemaphoreType.DMA((n,)),
            pltpu.SemaphoreType.DMA((tracers,)),
        ],
        compiler_params=pltpu.CompilerParams(collective_id=0, has_side_effects=True),
    )(
        field,
        *speeds,
        diffusivity.reshape(lons * blocks, LANES),
        cutoff,
        polar_mask,
        jnp.asarray(table),
        jnp.asarray(np.ascontiguousarray(table.transpose(0, 2, 1))),
    )
    result = result.reshape(tracers, lons, blocks, levels, LANES).transpose(0, 1, 3, 2, 4)
    return result.reshape(tracers, lons, levels, lat_rows).transpose(0, 2, 1, 3)


def solution(mesh):
    n = mesh.shape["lon"]
    members = mesh.shape["member"]
    placed = (
        P("member", None, "lon", None),
        P("member", "lon", None),
        P("member", "lon", None),
        P("member", "lon", None),
        P(),
        P(),
    )

    def run(tracer_field, *rest):
        tracers, levels, length, lat_rows = tracer_field.shape
        fits = (
            n == 2 * (tracers // members)
            and levels == 2
            and lat_rows % LANES == 0
            and (length // n) * (lat_rows // LANES) % 4 == 0
            and lat_rows // LANES <= 8
        )
        local = functools.partial(local_by_kernel, n) if fits else local_by_collectives
        return jax.shard_map(
            local, mesh=mesh, in_specs=placed, out_specs=P("member", None, "lon", None), check_vma=False
        )(tracer_field, *rest)

    return run
```

```python
import functools
import math

import jax
import jax.numpy as jnp
import numpy as np
from jax import lax
from jax.experimental import pallas as pl
from jax.experimental.layout import Layout, with_layout_constraint
from jax.experimental.pallas import tpu as pltpu
from jax.sharding import PartitionSpec as P

POLAR = 128
LANES = 128


def padded(x, sides, width):
    for axis, dim in sides:
        size, length = (lax.axis_size(axis), x.shape[dim])
        up = [(i, (i + 1) % size) for i in range(size)]
        down = [(j, i) for i, j in up]
        last = lax.slice_in_dim(x, length - width, length, axis=dim)
        leading = lax.slice_in_dim(x, 0, width, axis=dim)
        before = lax.ppermute(last, axis, up)
        after = lax.ppermute(leading, axis, down)
        x = jnp.concatenate([before, x, after], axis=dim)
    return x


def fourier_tables(length):
    half_len = length // 2
    column = jnp.arange(length, dtype=jnp.int32)[:, None]
    wavenum = jnp.arange(1, half_len + 1, dtype=jnp.int32)[None, :]
    phase = column * wavenum % length
    angle = 2.0 * math.pi / length * phase.astype(jnp.float32)
    return (jnp.cos(angle), jnp.sin(angle))


def high_part(block, row_cut, cosine, sine):
    length = block.shape[1]
    half_len = length // 2
    highest = lax.Precision.HIGHEST
    real_part = jnp.einsum("bir,im->brm", block, cosine, precision=highest)
    imag_part = jnp.einsum("bir,im->brm", block, sine, precision=highest)
    wavenum = jnp.arange(1, half_len + 1, dtype=jnp.int32)
    weights = jnp.where(wavenum == half_len, 1.0 / length, 2.0 / length).astype(jnp.float32)
    keeper = jnp.where(wavenum[None, :] > row_cut[:, None], weights[None, :], 0.0)
    return jnp.einsum(
        "brm,im->bir", real_part * keeper[None], cosine, precision=highest
    ) + jnp.einsum("brm,im->bir", imag_part * keeper[None], sine, precision=highest)


def local_by_collectives(tracer_field, courant_lon, courant_lat, diffusivity, polar_mask, cutoff):
    tracers, levels, lon_local, lat_rows = tracer_field.shape
    zero_row = jnp.zeros_like(tracer_field[..., :1])
    north_next = jnp.concatenate([tracer_field[..., 1:], zero_row], axis=3)
    north = (
        jnp.maximum(courant_lat, 0.0)[None] * tracer_field
        + jnp.minimum(courant_lat, 0.0)[None] * north_next
    )
    south = jnp.concatenate([zero_row, north[..., :-1]], axis=3)
    stacked = jnp.concatenate([tracer_field, courant_lon[None]], axis=0)
    extended = padded(stacked, (("lon", 2),), 1)
    tracer_ext = extended[:tracers]
    speed_ext = extended[tracers][None, :, :-1]
    east_all = (
        jnp.maximum(speed_ext, 0.0) * tracer_ext[:, :, :-1]
        + jnp.minimum(speed_ext, 0.0) * tracer_ext[:, :, 1:]
    )
    advected = tracer_field - (east_all[:, :, 1:] - east_all[:, :, :-1]) - (north - south)
    batched = advected.reshape(tracers * levels, lon_local, lat_rows)
    ends = jnp.concatenate([batched[..., :POLAR], batched[..., lat_rows - POLAR :]], axis=2)
    ends_mask = jnp.concatenate([polar_mask[:POLAR], polar_mask[lat_rows - POLAR :]])
    ends_cut = jnp.concatenate([cutoff[:POLAR], cutoff[lat_rows - POLAR :]])
    size = lax.axis_size("lon")
    cosine, sine = fourier_tables(lon_local * size)
    row_count = 2 * POLAR // size
    first_row = lax.axis_index("lon") * row_count
    my_cut = lax.dynamic_slice_in_dim(ends_cut, first_row, row_count)
    my_mask = lax.dynamic_slice_in_dim(ends_mask.astype(jnp.float32), first_row, row_count)
    removed = (
        high_part(
            lax.all_to_all(ends, "lon", split_axis=2, concat_axis=1, tiled=True),
            my_cut,
            cosine,
            sine,
        )
        * my_mask[None, None, :]
    )
    correction = lax.all_to_all(removed, "lon", split_axis=1, concat_axis=2, tiled=True)
    filtered = jnp.concatenate(
        [
            batched[..., :POLAR] - correction[..., :POLAR],
            batched[..., POLAR : lat_rows - POLAR],
            batched[..., lat_rows - POLAR :] - correction[..., POLAR:],
        ],
        axis=2,
    ).reshape(tracers, levels, lon_local, lat_rows)
    share = diffusivity[0] / (1.0 + 2.0 * diffusivity[0])
    moved = share[None] * (filtered[:, 1] - filtered[:, 0])
    return jnp.stack([filtered[:, 0] + moved, filtered[:, 1] - moved], axis=1)


def orthonormal_rows(length):
    half = length // 2
    wave = np.arange(1, half + 1)[:, None]
    angle = 2.0 * np.pi / length * (wave * np.arange(length)[None, :] % length)
    scale = np.sqrt(np.where(wave == half, 1.0, 2.0) / length)
    return np.concatenate([np.cos(angle) * scale, np.sin(angle) * scale], axis=0)


def split(x):
    high = x.astype(jnp.bfloat16)
    return high, (x - high.astype(jnp.float32)).astype(jnp.bfloat16)


def product(a_high, a_low, b):
    b_high, b_low = split(b)
    dot = functools.partial(jnp.dot, preferred_element_type=jnp.float32)
    return dot(a_high, b_high) + (dot(a_high, b_low) + dot(a_low, b_high))


def kernel(
    n, tracers, lons, blocks,
    t_hbm, c_hbm, cl_hbm, kd_hbm, cut_hbm, mask_hbm, g_hbm, gt_hbm, o_hbm,
    buf, clv, kv, cutv, maskv, gv, gtv, coef, adv, out_blocks, in_blocks, spec, back_blocks, corr,
    in_sem, halo_send, halo_recv, send_sem, recv_sem, back_send, back_recv, out_sem,
):
    rows = lons * blocks * 2
    stride = blocks * 2
    top = 16
    slot = spec.shape[0] // n
    me = lax.axis_index("lon")
    right, left = lax.rem(me + 1, n), lax.rem(me + n - 1, n)
    my_pair = me // 2
    half = lax.rem(me, 2)

    loads = [
        pltpu.make_async_copy(c_hbm, buf.at[tracers, pl.ds(top, rows)], in_sem.at[0]),
        pltpu.make_async_copy(cl_hbm, clv.at[pl.ds(8, rows)], in_sem.at[1]),
        pltpu.make_async_copy(t_hbm, buf.at[pl.ds(0, tracers), pl.ds(top, rows)], in_sem.at[2]),
        pltpu.make_async_copy(kd_hbm, kv, in_sem.at[3]),
        pltpu.make_async_copy(cut_hbm, cutv, in_sem.at[4]),
        pltpu.make_async_copy(mask_hbm, maskv, in_sem.at[5]),
        pltpu.make_async_copy(g_hbm, gv, in_sem.at[6]),
        pltpu.make_async_copy(gt_hbm, gtv, in_sem.at[7]),
    ]
    for load in loads:
        load.start()

    barrier = pltpu.get_barrier_semaphore()

    @pl.loop(1, n)
    def _(k):
        pl.semaphore_signal(barrier, inc=1, device_id={"lon": lax.rem(me + k, n)}, device_id_type=pl.DeviceIdType.MESH)

    pl.semaphore_wait(barrier, n - 1)

    def remote(src, dst, send, recv, to):
        return pltpu.make_async_remote_copy(
            src_ref=src, dst_ref=dst, send_sem=send, recv_sem=recv,
            device_id={"lon": to}, device_id_type=pl.DeviceIdType.MESH,
        )

    halos = [
        remote(c_hbm.at[pl.ds(rows - 16, 16)], buf.at[tracers, pl.ds(0, 16)], halo_send.at[0], halo_recv.at[0], right),
        remote(t_hbm.at[:, pl.ds(rows - 16, 16)], buf.at[pl.ds(0, tracers), pl.ds(0, 16)], halo_send.at[1], halo_recv.at[1], right),
        remote(t_hbm.at[:, pl.ds(0, 16)], buf.at[pl.ds(0, tracers), pl.ds(top + rows, 16)], halo_send.at[2], halo_recv.at[2], left),
    ]
    for halo in halos:
        halo.start()

    spec[...] = jnp.zeros_like(spec)
    clv[pl.ds(0, 8)] = jnp.zeros((8, LANES), jnp.float32)
    def factors(start, count):
        row = lax.rem(lax.broadcasted_iota(jnp.int32, (count, LANES), 0), stride)
        lane = lax.broadcasted_iota(jnp.int32, (count, LANES), 1)
        last_lane, first_lane = lane == LANES - 1, lane == 0
        here = pl.ds(start, count)
        cl = clv[pl.ds(8 + start, count)]
        cl_prev = pltpu.roll(jnp.where(last_lane, clv[pl.ds(6 + start, count)], cl), 1, axis=1)
        cl_prev = jnp.where((row < 2) & first_lane, 0.0, cl_prev)
        north_next = jnp.where((row >= stride - 2) & last_lane, 0.0, jnp.minimum(cl, 0.0))
        c = buf[tracers, pl.ds(top + start, count)]
        c_west = buf[tracers, pl.ds(top + start - stride, count)]
        rest = 1.0 - jnp.maximum(cl, 0.0) + jnp.minimum(cl_prev, 0.0)
        coef[0, here] = rest - jnp.maximum(c, 0.0) + jnp.minimum(c_west, 0.0)
        coef[1, here] = -jnp.minimum(c, 0.0)
        coef[2, here] = jnp.maximum(c_west, 0.0)
        coef[3, here] = -north_next
        coef[4, here] = jnp.maximum(cl_prev, 0.0)

    def advect(t, start, count):
        lane = lax.broadcasted_iota(jnp.int32, (count, LANES), 1)
        here = pl.ds(start, count)
        x = buf[t, pl.ds(top + start, count)]
        y = jnp.where(lane == 0, buf[t, pl.ds(top + start + 2, count)], x)
        total = coef[0, here] * x + coef[3, here] * pltpu.roll(y, LANES - 1, axis=1)
        y = jnp.where(lane == LANES - 1, buf[t, pl.ds(top + start - 2, count)], x)
        total += coef[4, here] * pltpu.roll(y, 1, axis=1)
        total += coef[1, here] * buf[t, pl.ds(top + start + stride, count)]
        total += coef[2, here] * buf[t, pl.ds(top + start - stride, count)]
        adv[t, here] = total

    early = 8
    late = lons - early
    cuts = ((0, stride), ((early + 1) * stride, (lons - early - 1) * stride))

    def cut_early(t):
        advect(t, stride, early * stride)
        for h in range(2):
            for lev in range(2):
                first = stride + h * (stride - 2) + lev
                out_blocks[2 * t + h, pl.ds(lev * early, early)] = adv[t, pl.ds(first, early, stride=stride)]

    def cut_late(t):
        for start, count in cuts:
            advect(t, start, count)
        for h in range(2):
            for lev in range(2):
                first = h * (stride - 2) + lev
                to = 2 * early + lev * late
                out_blocks[2 * t + h, pl.ds(to, late - 1)] = adv[t, pl.ds((early + 1) * stride + first, late - 1, stride=stride)]
                out_blocks[2 * t + h, pl.ds(to + late - 1, 1)] = adv[t, pl.ds(first, 1)]

    def pair_at(i):
        return lax.rem(my_pair + i + 1, tracers)

    parts = (pl.ds(0, 2 * early), pl.ds(2 * early, 2 * late))

    def send(dest, part):
        return remote(
            out_blocks.at[dest, parts[part]], in_blocks.at[me, parts[part]],
            send_sem.at[part, dest], recv_sem.at[part, me], dest,
        )

    twin = 2 * my_pair + 1 - half
    for load in loads[:3]:
        load.wait()
    factors(stride, early * stride)

    @pl.loop(0, tracers - 1)
    def _(i):
        t = pair_at(i)
        cut_early(t)
        send(2 * t, 0).start()
        send(2 * t + 1, 0).start()

    cut_early(my_pair)
    send(twin, 0).start()
    for halo in halos:
        halo.wait_recv()
    for start, count in cuts:
        factors(start, count)

    @pl.loop(0, tracers - 1)
    def _(i):
        t = pair_at(i)
        cut_late(t)
        send(2 * t, 1).start()
        send(2 * t + 1, 1).start()

    cut_late(my_pair)
    send(twin, 1).start()
    in_blocks[me] = out_blocks[me]

    loads[3].wait()
    k = kv[...]
    kv[...] = k / (1.0 + 2.0 * k)

    def solve(t, block, remove):
        share = kv[pl.ds(block, lons, stride=blocks)]
        at = [pl.ds(2 * block + lev, lons, stride=stride) for lev in range(2)]
        upper, lower = adv[t, at[0]], adv[t, at[1]]
        if remove is not None:
            upper = upper - corr[remove, pl.ds(0, lons)]
            lower = lower - corr[remove, pl.ds(lons, lons)]
        moved = share * (lower - upper)
        adv[t, at[0]] = upper + moved
        adv[t, at[1]] = lower - moved

    @pl.loop(0, tracers)
    def _(t):
        for block in range(1, blocks - 1):
            solve(t, block, None)

    for load in loads[4:]:
        load.wait()

    def receive(s):
        for part in range(2):
            remote(
                out_blocks.at[s, parts[part]], in_blocks.at[s, parts[part]],
                send_sem.at[part, s], recv_sem.at[part, s], s,
            ).wait_recv()

    def pack(s):
        first = pl.multiple_of(s * slot, slot)
        for lev in range(2):
            lanes = pl.ds(lev * LANES, LANES)
            spec[pl.ds(first, early), lanes] = in_blocks[s, pl.ds(lev * early, early)]
            spec[pl.ds(first + early, late), lanes] = in_blocks[s, pl.ds(2 * early + lev * late, late)]

    length = n * lons
    cut = jnp.where(half == 0, cutv[pl.ds(0, LANES)], cutv[pl.ds((blocks - 1) * LANES, LANES)])
    mask = jnp.where(half == 0, maskv[pl.ds(0, LANES)], maskv[pl.ds((blocks - 1) * LANES, LANES)])
    cut = jnp.where(mask == 1, cut, length).reshape(1, LANES)
    wave = lax.rem(lax.broadcasted_iota(jnp.int32, (length, LANES), 0), length // 2) + 1
    keep = wave > cut
    pack(me)
    receive(twin)
    pack(twin)

    @pl.loop(0, tracers - 1)
    def _(i):
        pair = pair_at(tracers - 2 - i)
        for h in range(2):
            receive(2 * pair + h)
            pack(2 * pair + h)

    waves = product(gv[0], gv[1], spec[...])
    waves = jnp.where(jnp.concatenate([keep, keep], axis=1), waves, 0.0)
    spec[...] = product(gtv[0], gtv[1], waves)
    def unpack(s):
        first = pl.multiple_of(s * slot, slot)
        for lev in range(2):
            back_blocks[s, pl.ds(lev * lons, lons)] = spec[pl.ds(first, lons), pl.ds(lev * LANES, LANES)]

    def back(dest):
        return remote(back_blocks.at[dest], corr.at[me], back_send.at[dest], back_recv.at[me], dest)

    @pl.loop(0, tracers - 1)
    def _(i):
        pair = pair_at(i)
        for h in range(2):
            unpack(2 * pair + h)
            back(2 * pair + h).start()

    unpack(twin)
    back(twin).start()
    unpack(me)

    corr[me] = back_blocks[me]

    def returned(s):
        return remote(back_blocks.at[s], corr.at[s], back_send.at[s], back_recv.at[s], s)

    def finish(t):
        solve(t, 0, 2 * t)
        solve(t, blocks - 1, 2 * t + 1)
        pltpu.make_async_copy(adv.at[t], o_hbm.at[t], out_sem.at[t]).start()

    returned(twin).wait_recv()
    finish(my_pair)

    @pl.loop(0, tracers - 1)
    def _(i):
        t = pair_at(tracers - 2 - i)
        returned(2 * t).wait_recv()
        returned(2 * t + 1).wait_recv()
        finish(t)

    for halo in halos:
        halo.wait_send()

    @pl.loop(1, n)
    def _(k):
        dest = lax.rem(me + k, n)
        send(dest, 0).wait_send()
        send(dest, 1).wait_send()
        back(dest).wait_send()

    @pl.loop(0, tracers)
    def _(t):
        pltpu.make_async_copy(adv.at[t], o_hbm.at[t], out_sem.at[t]).wait()


def flat_rows(x):
    count, levels, lons, lat_rows = x.shape
    x = x.transpose(0, 2, 1, 3).reshape(count, lons, levels, lat_rows // LANES, LANES)
    x = with_layout_constraint(x, Layout((0, 1, 3, 2, 4)))
    return x.transpose(0, 1, 3, 2, 4).reshape(count, lons * lat_rows // LANES * levels, LANES)


def local_by_kernel(n, tracer_field, courant_lon, courant_lat, diffusivity, polar_mask, cutoff):
    tracers, levels, lons, lat_rows = tracer_field.shape
    blocks = lat_rows // LANES
    rows = lons * blocks * levels
    field = flat_rows(tracer_field)
    speeds = [flat_rows(x[None])[0] for x in (courant_lon, courant_lat)]
    length = n * lons
    g = orthonormal_rows(length).astype(np.float32)
    slot = -(-lons // 8) * 8
    tables = []
    for order in ([*range(1, lons), 0], [*range(lons)]):
        wide = np.zeros((length, n, slot), np.float32)
        wide[:, :, :lons] = g.reshape(length, n, lons)[:, :, order]
        wide = wide.reshape(length, n * slot)
        high = wide.astype(jnp.bfloat16)
        tables.append(np.stack([high, (wide - high.astype(np.float32)).astype(jnp.bfloat16)]))
    f32 = jnp.float32
    result = pl.pallas_call(
        functools.partial(kernel, n, tracers, lons, blocks),
        out_shape=jax.ShapeDtypeStruct((tracers, rows, LANES), f32),
        in_specs=[pl.BlockSpec(memory_space=pl.ANY)] * 8,
        out_specs=pl.BlockSpec(memory_space=pl.ANY),
        scratch_shapes=[
            pltpu.VMEM((tracers + 1, rows + 32, LANES), f32),
            pltpu.VMEM((rows + 8, LANES), f32),
            pltpu.VMEM((lons * blocks, LANES), f32),
            pltpu.VMEM((lat_rows,), jnp.int32),
            pltpu.VMEM((lat_rows,), jnp.int32),
            pltpu.VMEM((2, length, n * slot), jnp.bfloat16),
            pltpu.VMEM((2, n * slot, length), jnp.bfloat16),
            pltpu.VMEM((5, rows, LANES), f32),
            pltpu.VMEM((tracers, rows, LANES), f32),
            pltpu.VMEM((n, 2 * lons, LANES), f32),
            pltpu.VMEM((n, 2 * lons, LANES), f32),
            pltpu.VMEM((n * slot, 2 * LANES), f32),
            pltpu.VMEM((n, 2 * lons, LANES), f32),
            pltpu.VMEM((n, 2 * lons, LANES), f32),
            pltpu.SemaphoreType.DMA((8,)),
            pltpu.SemaphoreType.DMA((3,)),
            pltpu.SemaphoreType.DMA((3,)),
            pltpu.SemaphoreType.DMA((2, n)),
            pltpu.SemaphoreType.DMA((2, n)),
            pltpu.SemaphoreType.DMA((n,)),
            pltpu.SemaphoreType.DMA((n,)),
            pltpu.SemaphoreType.DMA((tracers,)),
        ],
        compiler_params=pltpu.CompilerParams(collective_id=0, has_side_effects=True),
    )(
        field,
        *speeds,
        diffusivity.reshape(lons * blocks, LANES),
        cutoff,
        polar_mask,
        jnp.asarray(tables[0]),
        jnp.asarray(np.ascontiguousarray(tables[1].transpose(0, 2, 1))),
    )
    result = result.reshape(tracers, lons, blocks, levels, LANES).transpose(0, 1, 3, 2, 4)
    return result.reshape(tracers, lons, levels, lat_rows).transpose(0, 2, 1, 3)


def solution(mesh):
    n = mesh.shape["lon"]
    members = mesh.shape["member"]
    placed = (
        P("member", None, "lon", None),
        P("member", "lon", None),
        P("member", "lon", None),
        P("member", "lon", None),
        P(),
        P(),
    )

    def run(tracer_field, *rest):
        tracers, levels, length, lat_rows = tracer_field.shape
        fits = (
            n == 2 * (tracers // members)
            and levels == 2
            and lat_rows % LANES == 0
            and length == 12 * n
            and lat_rows // LANES <= 8
        )
        local = functools.partial(local_by_kernel, n) if fits else local_by_collectives
        return jax.shard_map(
            local, mesh=mesh, in_specs=placed, out_specs=P("member", None, "lon", None), check_vma=False
        )(tracer_field, *rest)

    return run
```

```python
import functools
import math

import jax
import jax.numpy as jnp
import numpy as np
from jax import lax
from jax.experimental import pallas as pl
from jax.experimental.layout import Layout, with_layout_constraint
from jax.experimental.pallas import tpu as pltpu
from jax.sharding import PartitionSpec as P

POLAR = 128
LANES = 128


def padded(x, sides, width):
    for axis, dim in sides:
        size, length = (lax.axis_size(axis), x.shape[dim])
        up = [(i, (i + 1) % size) for i in range(size)]
        down = [(j, i) for i, j in up]
        last = lax.slice_in_dim(x, length - width, length, axis=dim)
        leading = lax.slice_in_dim(x, 0, width, axis=dim)
        before = lax.ppermute(last, axis, up)
        after = lax.ppermute(leading, axis, down)
        x = jnp.concatenate([before, x, after], axis=dim)
    return x


def fourier_tables(length):
    half_len = length // 2
    column = jnp.arange(length, dtype=jnp.int32)[:, None]
    wavenum = jnp.arange(1, half_len + 1, dtype=jnp.int32)[None, :]
    phase = column * wavenum % length
    angle = 2.0 * math.pi / length * phase.astype(jnp.float32)
    return (jnp.cos(angle), jnp.sin(angle))


def high_part(block, row_cut, cosine, sine):
    length = block.shape[1]
    half_len = length // 2
    highest = lax.Precision.HIGHEST
    real_part = jnp.einsum("bir,im->brm", block, cosine, precision=highest)
    imag_part = jnp.einsum("bir,im->brm", block, sine, precision=highest)
    wavenum = jnp.arange(1, half_len + 1, dtype=jnp.int32)
    weights = jnp.where(wavenum == half_len, 1.0 / length, 2.0 / length).astype(jnp.float32)
    keeper = jnp.where(wavenum[None, :] > row_cut[:, None], weights[None, :], 0.0)
    return jnp.einsum(
        "brm,im->bir", real_part * keeper[None], cosine, precision=highest
    ) + jnp.einsum("brm,im->bir", imag_part * keeper[None], sine, precision=highest)


def local_by_collectives(tracer_field, courant_lon, courant_lat, diffusivity, polar_mask, cutoff):
    tracers, levels, lon_local, lat_rows = tracer_field.shape
    zero_row = jnp.zeros_like(tracer_field[..., :1])
    north_next = jnp.concatenate([tracer_field[..., 1:], zero_row], axis=3)
    north = (
        jnp.maximum(courant_lat, 0.0)[None] * tracer_field
        + jnp.minimum(courant_lat, 0.0)[None] * north_next
    )
    south = jnp.concatenate([zero_row, north[..., :-1]], axis=3)
    stacked = jnp.concatenate([tracer_field, courant_lon[None]], axis=0)
    extended = padded(stacked, (("lon", 2),), 1)
    tracer_ext = extended[:tracers]
    speed_ext = extended[tracers][None, :, :-1]
    east_all = (
        jnp.maximum(speed_ext, 0.0) * tracer_ext[:, :, :-1]
        + jnp.minimum(speed_ext, 0.0) * tracer_ext[:, :, 1:]
    )
    advected = tracer_field - (east_all[:, :, 1:] - east_all[:, :, :-1]) - (north - south)
    batched = advected.reshape(tracers * levels, lon_local, lat_rows)
    ends = jnp.concatenate([batched[..., :POLAR], batched[..., lat_rows - POLAR :]], axis=2)
    ends_mask = jnp.concatenate([polar_mask[:POLAR], polar_mask[lat_rows - POLAR :]])
    ends_cut = jnp.concatenate([cutoff[:POLAR], cutoff[lat_rows - POLAR :]])
    size = lax.axis_size("lon")
    cosine, sine = fourier_tables(lon_local * size)
    row_count = 2 * POLAR // size
    first_row = lax.axis_index("lon") * row_count
    my_cut = lax.dynamic_slice_in_dim(ends_cut, first_row, row_count)
    my_mask = lax.dynamic_slice_in_dim(ends_mask.astype(jnp.float32), first_row, row_count)
    removed = (
        high_part(
            lax.all_to_all(ends, "lon", split_axis=2, concat_axis=1, tiled=True),
            my_cut,
            cosine,
            sine,
        )
        * my_mask[None, None, :]
    )
    correction = lax.all_to_all(removed, "lon", split_axis=1, concat_axis=2, tiled=True)
    filtered = jnp.concatenate(
        [
            batched[..., :POLAR] - correction[..., :POLAR],
            batched[..., POLAR : lat_rows - POLAR],
            batched[..., lat_rows - POLAR :] - correction[..., POLAR:],
        ],
        axis=2,
    ).reshape(tracers, levels, lon_local, lat_rows)
    share = diffusivity[0] / (1.0 + 2.0 * diffusivity[0])
    moved = share[None] * (filtered[:, 1] - filtered[:, 0])
    return jnp.stack([filtered[:, 0] + moved, filtered[:, 1] - moved], axis=1)


def orthonormal_rows(length):
    half = length // 2
    wave = np.arange(1, half + 1)[:, None]
    angle = 2.0 * np.pi / length * (wave * np.arange(length)[None, :] % length)
    scale = np.sqrt(np.where(wave == half, 1.0, 2.0) / length)
    return np.concatenate([np.cos(angle) * scale, np.sin(angle) * scale], axis=0)


def split(x):
    high = x.astype(jnp.bfloat16)
    return high, (x - high.astype(jnp.float32)).astype(jnp.bfloat16)


def product(a_high, a_low, b):
    b_high, b_low = split(b)
    dot = functools.partial(jnp.dot, preferred_element_type=jnp.float32)
    return dot(a_high, b_high) + (dot(a_high, b_low) + dot(a_low, b_high))


def kernel(
    n, tracers, lons, blocks,
    t_hbm, c_hbm, cl_hbm, kd_hbm, cut_hbm, mask_hbm, g_hbm, gt_hbm, o_hbm,
    buf, clv, kv, cutv, maskv, gv, gtv, coef, adv, out_blocks, in_blocks, spec, back_blocks, corr,
    in_sem, halo_send, halo_recv, send_sem, recv_sem, back_send, back_recv, out_sem,
):
    rows = lons * blocks * 2
    stride = blocks * 2
    top = 16
    slot = spec.shape[0] // n
    me = lax.axis_index("lon")
    right, left = lax.rem(me + 1, n), lax.rem(me + n - 1, n)
    my_pair = me // 2
    half = lax.rem(me, 2)

    loads = [
        pltpu.make_async_copy(c_hbm, buf.at[tracers, pl.ds(top, rows)], in_sem.at[0]),
        pltpu.make_async_copy(cl_hbm, clv.at[pl.ds(8, rows)], in_sem.at[1]),
        pltpu.make_async_copy(t_hbm, buf.at[pl.ds(0, tracers), pl.ds(top, rows)], in_sem.at[2]),
        pltpu.make_async_copy(kd_hbm, kv, in_sem.at[3]),
        pltpu.make_async_copy(cut_hbm, cutv, in_sem.at[4]),
        pltpu.make_async_copy(mask_hbm, maskv, in_sem.at[5]),
        pltpu.make_async_copy(g_hbm, gv, in_sem.at[6]),
        pltpu.make_async_copy(gt_hbm, gtv, in_sem.at[7]),
    ]
    for load in loads:
        load.start()

    barrier = pltpu.get_barrier_semaphore()

    @pl.loop(1, n)
    def _(k):
        pl.semaphore_signal(barrier, inc=1, device_id={"lon": lax.rem(me + k, n)}, device_id_type=pl.DeviceIdType.MESH)

    def remote(src, dst, send, recv, to):
        return pltpu.make_async_remote_copy(
            src_ref=src, dst_ref=dst, send_sem=send, recv_sem=recv,
            device_id={"lon": to}, device_id_type=pl.DeviceIdType.MESH,
        )

    halos = [
        remote(c_hbm.at[pl.ds(rows - 16, 16)], buf.at[tracers, pl.ds(0, 16)], halo_send.at[0], halo_recv.at[0], right),
        remote(t_hbm.at[:, pl.ds(rows - 16, 16)], buf.at[pl.ds(0, tracers), pl.ds(0, 16)], halo_send.at[1], halo_recv.at[1], right),
        remote(t_hbm.at[:, pl.ds(0, 16)], buf.at[pl.ds(0, tracers), pl.ds(top + rows, 16)], halo_send.at[2], halo_recv.at[2], left),
    ]
    spec[...] = jnp.zeros_like(spec)
    clv[pl.ds(0, 8)] = jnp.zeros((8, LANES), jnp.float32)
    def factors(start, count):
        row = lax.rem(lax.broadcasted_iota(jnp.int32, (count, LANES), 0), stride)
        lane = lax.broadcasted_iota(jnp.int32, (count, LANES), 1)
        last_lane, first_lane = lane == LANES - 1, lane == 0
        here = pl.ds(start, count)
        cl = clv[pl.ds(8 + start, count)]
        cl_prev = pltpu.roll(jnp.where(last_lane, clv[pl.ds(6 + start, count)], cl), 1, axis=1)
        cl_prev = jnp.where((row < 2) & first_lane, 0.0, cl_prev)
        north_next = jnp.where((row >= stride - 2) & last_lane, 0.0, jnp.minimum(cl, 0.0))
        c = buf[tracers, pl.ds(top + start, count)]
        c_west = buf[tracers, pl.ds(top + start - stride, count)]
        rest = 1.0 - jnp.maximum(cl, 0.0) + jnp.minimum(cl_prev, 0.0)
        coef[0, here] = rest - jnp.maximum(c, 0.0) + jnp.minimum(c_west, 0.0)
        coef[1, here] = -jnp.minimum(c, 0.0)
        coef[2, here] = jnp.maximum(c_west, 0.0)
        coef[3, here] = -north_next
        coef[4, here] = jnp.maximum(cl_prev, 0.0)

    def advect(t, start, count):
        lane = lax.broadcasted_iota(jnp.int32, (count, LANES), 1)
        here = pl.ds(start, count)
        x = buf[t, pl.ds(top + start, count)]
        y = jnp.where(lane == 0, buf[t, pl.ds(top + start + 2, count)], x)
        total = coef[0, here] * x + coef[3, here] * pltpu.roll(y, LANES - 1, axis=1)
        y = jnp.where(lane == LANES - 1, buf[t, pl.ds(top + start - 2, count)], x)
        total += coef[4, here] * pltpu.roll(y, 1, axis=1)
        total += coef[1, here] * buf[t, pl.ds(top + start + stride, count)]
        total += coef[2, here] * buf[t, pl.ds(top + start - stride, count)]
        adv[t, here] = total

    early = 8
    late = lons - early
    cuts = ((0, stride), ((early + 1) * stride, (lons - early - 1) * stride))

    def cut_early(t):
        advect(t, stride, early * stride)
        for h in range(2):
            for lev in range(2):
                first = stride + h * (stride - 2) + lev
                out_blocks[2 * t + h, pl.ds(lev * early, early)] = adv[t, pl.ds(first, early, stride=stride)]

    def cut_late(t):
        for start, count in cuts:
            advect(t, start, count)
        for h in range(2):
            for lev in range(2):
                first = h * (stride - 2) + lev
                to = 2 * early + lev * late
                out_blocks[2 * t + h, pl.ds(to, late - 1)] = adv[t, pl.ds((early + 1) * stride + first, late - 1, stride=stride)]
                out_blocks[2 * t + h, pl.ds(to + late - 1, 1)] = adv[t, pl.ds(first, 1)]

    def pair_at(i):
        return lax.rem(my_pair + i + 1, tracers)

    parts = (pl.ds(0, 2 * early), pl.ds(2 * early, 2 * late))

    def send(dest, part):
        return remote(
            out_blocks.at[dest, parts[part]], in_blocks.at[me, parts[part]],
            send_sem.at[part, dest], recv_sem.at[part, me], dest,
        )

    twin = 2 * my_pair + 1 - half
    for load in loads[:3]:
        load.wait()
    factors(stride, early * stride)

    @pl.loop(0, tracers)
    def _(t):
        cut_early(t)

    pl.semaphore_wait(barrier, n - 1)
    for halo in halos:
        halo.start()

    @pl.loop(0, tracers - 1)
    def _(i):
        t = pair_at(i)
        send(2 * t, 0).start()
        send(2 * t + 1, 0).start()

    send(twin, 0).start()
    for halo in halos:
        halo.wait_recv()
    for start, count in cuts:
        factors(start, count)

    @pl.loop(0, tracers - 1)
    def _(i):
        t = pair_at(i)
        cut_late(t)
        send(2 * t, 1).start()
        send(2 * t + 1, 1).start()

    cut_late(my_pair)
    send(twin, 1).start()
    in_blocks[me] = out_blocks[me]

    loads[3].wait()
    k = kv[...]
    kv[...] = k / (1.0 + 2.0 * k)

    def solve(t, block, remove):
        share = kv[pl.ds(block, lons, stride=blocks)]
        at = [pl.ds(2 * block + lev, lons, stride=stride) for lev in range(2)]
        upper, lower = adv[t, at[0]], adv[t, at[1]]
        if remove is not None:
            upper = upper - corr[remove, pl.ds(0, lons)]
            lower = lower - corr[remove, pl.ds(lons, lons)]
        moved = share * (lower - upper)
        adv[t, at[0]] = upper + moved
        adv[t, at[1]] = lower - moved

    @pl.loop(0, tracers)
    def _(t):
        for block in range(1, blocks - 1):
            solve(t, block, None)

    for load in loads[4:]:
        load.wait()

    def receive(s):
        for part in range(2):
            remote(
                out_blocks.at[s, parts[part]], in_blocks.at[s, parts[part]],
                send_sem.at[part, s], recv_sem.at[part, s], s,
            ).wait_recv()

    def pack(s):
        first = pl.multiple_of(s * slot, slot)
        for lev in range(2):
            lanes = pl.ds(lev * LANES, LANES)
            spec[pl.ds(first, early), lanes] = in_blocks[s, pl.ds(lev * early, early)]
            spec[pl.ds(first + early, late), lanes] = in_blocks[s, pl.ds(2 * early + lev * late, late)]

    length = n * lons
    cut = jnp.where(half == 0, cutv[pl.ds(0, LANES)], cutv[pl.ds((blocks - 1) * LANES, LANES)])
    mask = jnp.where(half == 0, maskv[pl.ds(0, LANES)], maskv[pl.ds((blocks - 1) * LANES, LANES)])
    cut = jnp.where(mask == 1, cut, length).reshape(1, LANES)
    wave = lax.rem(lax.broadcasted_iota(jnp.int32, (length, LANES), 0), length // 2) + 1
    keep = wave > cut
    pack(me)
    receive(twin)
    pack(twin)

    @pl.loop(0, tracers - 1)
    def _(i):
        pair = pair_at(tracers - 2 - i)
        for h in range(2):
            receive(2 * pair + h)
            pack(2 * pair + h)

    waves = product(gv[0], gv[1], spec[...])
    waves = jnp.where(jnp.concatenate([keep, keep], axis=1), waves, 0.0)
    spec[...] = product(gtv[0], gtv[1], waves)
    def unpack(s):
        first = pl.multiple_of(s * slot, slot)
        for lev in range(2):
            back_blocks[s, pl.ds(lev * lons, lons)] = spec[pl.ds(first, lons), pl.ds(lev * LANES, LANES)]

    def back(dest):
        return remote(back_blocks.at[dest], corr.at[me], back_send.at[dest], back_recv.at[me], dest)

    @pl.loop(0, tracers - 1)
    def _(i):
        pair = pair_at(i)
        for h in range(2):
            unpack(2 * pair + h)
            back(2 * pair + h).start()

    unpack(twin)
    back(twin).start()
    unpack(me)

    corr[me] = back_blocks[me]

    def returned(s):
        return remote(back_blocks.at[s], corr.at[s], back_send.at[s], back_recv.at[s], s)

    def finish(t):
        solve(t, 0, 2 * t)
        solve(t, blocks - 1, 2 * t + 1)
        pltpu.make_async_copy(adv.at[t], o_hbm.at[t], out_sem.at[t]).start()

    returned(twin).wait_recv()
    finish(my_pair)

    @pl.loop(0, tracers - 1)
    def _(i):
        t = pair_at(tracers - 2 - i)
        returned(2 * t).wait_recv()
        returned(2 * t + 1).wait_recv()
        finish(t)

    for halo in halos:
        halo.wait_send()

    @pl.loop(1, n)
    def _(k):
        dest = lax.rem(me + k, n)
        send(dest, 0).wait_send()
        send(dest, 1).wait_send()
        back(dest).wait_send()

    @pl.loop(0, tracers)
    def _(t):
        pltpu.make_async_copy(adv.at[t], o_hbm.at[t], out_sem.at[t]).wait()


def flat_rows(x):
    count, levels, lons, lat_rows = x.shape
    x = x.transpose(0, 2, 1, 3).reshape(count, lons, levels, lat_rows // LANES, LANES)
    x = with_layout_constraint(x, Layout((0, 1, 3, 2, 4)))
    return x.transpose(0, 1, 3, 2, 4).reshape(count, lons * lat_rows // LANES * levels, LANES)


def local_by_kernel(n, tracer_field, courant_lon, courant_lat, diffusivity, polar_mask, cutoff):
    tracers, levels, lons, lat_rows = tracer_field.shape
    blocks = lat_rows // LANES
    rows = lons * blocks * levels
    field = flat_rows(tracer_field)
    speeds = [flat_rows(x[None])[0] for x in (courant_lon, courant_lat)]
    length = n * lons
    g = orthonormal_rows(length).astype(np.float32)
    slot = -(-lons // 8) * 8
    tables = []
    for order in ([*range(1, lons), 0], [*range(lons)]):
        wide = np.zeros((length, n, slot), np.float32)
        wide[:, :, :lons] = g.reshape(length, n, lons)[:, :, order]
        wide = wide.reshape(length, n * slot)
        high = wide.astype(jnp.bfloat16)
        tables.append(np.stack([high, (wide - high.astype(np.float32)).astype(jnp.bfloat16)]))
    f32 = jnp.float32
    result = pl.pallas_call(
        functools.partial(kernel, n, tracers, lons, blocks),
        out_shape=jax.ShapeDtypeStruct((tracers, rows, LANES), f32),
        in_specs=[pl.BlockSpec(memory_space=pl.ANY)] * 8,
        out_specs=pl.BlockSpec(memory_space=pl.ANY),
        scratch_shapes=[
            pltpu.VMEM((tracers + 1, rows + 32, LANES), f32),
            pltpu.VMEM((rows + 8, LANES), f32),
            pltpu.VMEM((lons * blocks, LANES), f32),
            pltpu.VMEM((lat_rows,), jnp.int32),
            pltpu.VMEM((lat_rows,), jnp.int32),
            pltpu.VMEM((2, length, n * slot), jnp.bfloat16),
            pltpu.VMEM((2, n * slot, length), jnp.bfloat16),
            pltpu.VMEM((5, rows, LANES), f32),
            pltpu.VMEM((tracers, rows, LANES), f32),
            pltpu.VMEM((n, 2 * lons, LANES), f32),
            pltpu.VMEM((n, 2 * lons, LANES), f32),
            pltpu.VMEM((n * slot, 2 * LANES), f32),
            pltpu.VMEM((n, 2 * lons, LANES), f32),
            pltpu.VMEM((n, 2 * lons, LANES), f32),
            pltpu.SemaphoreType.DMA((8,)),
            pltpu.SemaphoreType.DMA((3,)),
            pltpu.SemaphoreType.DMA((3,)),
            pltpu.SemaphoreType.DMA((2, n)),
            pltpu.SemaphoreType.DMA((2, n)),
            pltpu.SemaphoreType.DMA((n,)),
            pltpu.SemaphoreType.DMA((n,)),
            pltpu.SemaphoreType.DMA((tracers,)),
        ],
        compiler_params=pltpu.CompilerParams(collective_id=0, has_side_effects=True),
    )(
        field,
        *speeds,
        diffusivity.reshape(lons * blocks, LANES),
        cutoff,
        polar_mask,
        jnp.asarray(tables[0]),
        jnp.asarray(np.ascontiguousarray(tables[1].transpose(0, 2, 1))),
    )
    result = result.reshape(tracers, lons, blocks, levels, LANES).transpose(0, 1, 3, 2, 4)
    return result.reshape(tracers, lons, levels, lat_rows).transpose(0, 2, 1, 3)


def solution(mesh):
    n = mesh.shape["lon"]
    members = mesh.shape["member"]
    placed = (
        P("member", None, "lon", None),
        P("member", "lon", None),
        P("member", "lon", None),
        P("member", "lon", None),
        P(),
        P(),
    )

    def run(tracer_field, *rest):
        tracers, levels, length, lat_rows = tracer_field.shape
        fits = (
            n == 2 * (tracers // members)
            and levels == 2
            and lat_rows % LANES == 0
            and length == 12 * n
            and lat_rows // LANES <= 8
        )
        local = functools.partial(local_by_kernel, n) if fits else local_by_collectives
        return jax.shard_map(
            local, mesh=mesh, in_specs=placed, out_specs=P("member", None, "lon", None), check_vma=False
        )(tracer_field, *rest)

    return run
```
